32 devices in a mesh: groups: 2 (over y), lat: 4 (over z), lon: 2 (over x), lev: 2 (over core).
Axes of the slice: x: 2, y: 2, z: 4, core: 2. Of those that a mesh axis runs over, the one named last changes fastest.
Arguments:
- model_field: bfloat16 [16, 128, 4, 2, 1024], P('groups', 'lev', 'lat', 'lon'), parts along dimension 0, may hold values from -6 to 6
- interp_weights: bfloat16 [4, 2, 8, 2, 128, 128], P('lat', 'lon'), may hold values from -0.375 to 0.375
- interp_blocks: int32 [4, 2, 8, 2], P('lat', 'lon'), may hold values from 0 to 7
- send_list: int32 [4, 2, 2], P('lat', 'lon'), may hold values from 0 to 7
- send_count: int32 [4, 2], P('lat', 'lon'), may hold values from 1 to 2
- conv_weights: bfloat16 [4, 2, 8, 10, 128, 128], P('lat', 'lon'), may hold values from -0.15625 to 0.15625
- neighbours: int32 [4, 2, 8, 10], P('lat', 'lon'), may hold values from 0 to 37
Outputs:
- subgrid_field: bfloat16 [16, 128, 4, 2, 1024], P('groups', 'lev', 'lat', 'lon'), parts along dimension 0
The draws below stay inside these ranges and needn't reach their ends.
There are 2 independent parts, one for each index of `groups`. The reference program is written for one: setup_inputs(seed, part) draws one part's arguments, and reference() takes and returns one part's arrays. A program takes and returns all parts, laid end to end along the dimension named above; an argument that names none is the same for every part. Nothing has to cross between parts.
All inputs are finite; a program needn't handle non-finite values.
Results may differ from the reference program's by a relative error of at most 0.0049.
Values may be sent and summed in bfloat16 or wider, within the bound.
A program may use at most 64 MiB of HBM per device.

```python
import jax
import jax.numpy as jnp
from jax import lax

M = 8
LEV = 128
BLK = 128
CB = 8
SB = 8
Q = 2
J = 10
HS = 2
E = 38
N_LAT = 4
N_LON = 2


def plant(values, own_key, low, high):
    spot = [jax.random.randint(jax.random.fold_in(own_key, axis), (), 0, length) for axis, length in enumerate(values.shape)]
    main_axis = values.shape.index(max(values.shape))
    next_to = spot[:main_axis] + [(spot[main_axis] + 1) % values.shape[main_axis]] + spot[main_axis + 1:]
    return values.at[tuple(spot)].set(low).at[tuple(next_to)].set(high)


def block_levels(rng, shape, cuts, least, top_value):
    loudness = 1.0
    for axis_at, shards_of in cuts:
        steps = jax.random.uniform(jax.random.fold_in(jax.random.fold_in(rng, 6), axis_at), (shards_of,), jnp.float32, least / len(cuts), top_value / len(cuts))
        loudness = loudness * jnp.repeat(jnp.exp(steps), shape[axis_at] // shards_of).reshape((-1,) + (1,) * (len(shape) - 1 - axis_at))
    return loudness


def normal_values(stream_key, dims, deviation, reach, cuts=(), kind=jnp.bfloat16):
    array = deviation * jax.random.normal(stream_key, dims, jnp.float32)
    if cuts:
        array = array * block_levels(stream_key, dims, cuts, -0.22, 0.18)
    return jnp.clip(array, -reach, reach).astype(kind)


def setup_inputs(seed: int = 0, part: int = 0) -> dict:
    key_of = jax.random.split(jax.random.key(seed), 8)
    part_splits = jax.random.split(jax.random.fold_in(key_of[7], part), 8)
    return {
        "model_field": normal_values(part_splits[0], (M, LEV, N_LAT, N_LON, CB * BLK), 1.0, 6.0, ((1, 2), (2, 4), (3, 2))),
        "interp_weights": normal_values(key_of[1], (N_LAT, N_LON, SB, Q, BLK, BLK), (Q * BLK) ** -0.5, 0.375, ((0, 4), (1, 2))),
        "interp_blocks": plant(jax.random.randint(key_of[2], (N_LAT, N_LON, SB, Q), 0, CB), jax.random.fold_in(key_of[2], 1), 0, CB - 1).astype(jnp.int32),
        "send_list": plant(jax.random.randint(key_of[3], (N_LAT, N_LON, HS), 0, SB), jax.random.fold_in(key_of[3], 1), 0, SB - 1).astype(jnp.int32),
        "send_count": plant(jax.random.randint(key_of[4], (N_LAT, N_LON), 1, HS + 1), jax.random.fold_in(key_of[4], 1), 1, HS).astype(jnp.int32),
        "conv_weights": normal_values(key_of[5], (N_LAT, N_LON, SB, J, BLK, BLK), (J * BLK) ** -0.5, 0.15625, ((0, 4), (1, 2))),
        "neighbours": plant(jax.random.randint(key_of[6], (N_LAT, N_LON, SB, J), 0, E), jax.random.fold_in(key_of[6], 1), 0, E - 1).astype(jnp.int32),
    }


def reference(model_field, interp_weights, interp_blocks, send_list, send_count, conv_weights, neighbours):
    cells = model_field.reshape(M, LEV, N_LAT, N_LON, CB, BLK)
    by_band = jnp.moveaxis(cells, 2, 0)

    def interp_band(inputs):
        band_cells, band_weights, band_blocks = inputs
        picked = jax.vmap(lambda part, which: part[:, :, which, :], in_axes=(2, 0), out_axes=2)(band_cells, band_blocks)
        total = jnp.einsum('mlnkqc,nkqcd->mlnkd', picked.astype(jnp.float32), band_weights.astype(jnp.float32))
        return total.astype(jnp.bfloat16)

    sub = lax.map(interp_band, (by_band, interp_weights, interp_blocks))

    def pack_band(band_sub, band_list):
        return jax.vmap(lambda part, which: part[:, :, which, :], in_axes=(2, 0), out_axes=2)(band_sub, band_list)

    chosen = jax.vmap(pack_band)(sub, send_list)
    live = jnp.arange(HS, dtype=jnp.int32)[None, None, :] < send_count[:, :, None]
    packed = jnp.where(live[:, None, None, :, :, None], chosen, jnp.zeros((), jnp.bfloat16))
    padded = jnp.pad(packed, ((2, 2), (0, 0), (0, 0), (0, 0), (0, 0), (0, 0)))

    def conv_band(inputs):
        band, band_sub, band_weights, band_nbrs = inputs
        pieces = [band_sub]
        for offset_a in (0, 1, 2, -1, -2):
            rows = lax.dynamic_index_in_dim(padded, band + 2 - offset_a, 0, keepdims=False)
            for offset_b in (0, 1, -1):
                pieces.append(jnp.roll(rows, offset_b, axis=2))
        readable = jnp.concatenate(pieces, axis=3)
        picked = jax.vmap(lambda part, which: part[:, :, which, :], in_axes=(2, 0), out_axes=2)(readable, band_nbrs)
        total = jnp.einsum('mlnkjc,nkjcd->mlnkd', picked.astype(jnp.float32), band_weights.astype(jnp.float32))
        return total.astype(jnp.bfloat16)

    bands = jnp.arange(N_LAT, dtype=jnp.int32)
    result = lax.map(conv_band, (bands, sub, conv_weights, neighbours))
    result = jnp.moveaxis(result, 0, 2)
    return result.reshape(M, LEV, N_LAT, N_LON, SB * BLK)
```

```python
import functools

import jax
import jax.numpy as jnp
from jax import lax
from jax.experimental import pallas as pl
from jax.experimental.pallas import tpu as pltpu
from jax.sharding import PartitionSpec as P

MESH = pl.DeviceIdType.MESH
STEPS = (0, 1, 2, -1, -2)
CHUNKS = 4


def kernel(
    n_lat,
    n_lon,
    sides,
    blocks_ref,
    list_ref,
    count_ref,
    near_ref,
    field_hbm,
    interp_hbm,
    conv_hbm,
    out_hbm,
    field,
    interp,
    conv,
    out,
    field_sem,
    weight_sem,
    out_sem,
    send_sem,
    recv_sem,
    *readable,
):
    chunks = len(readable)
    width = interp.shape[-1]
    tiles = interp.shape[0]
    joins = conv.shape[1] // width
    feeds = interp.shape[1] // width
    slots = list_ref.shape[1]
    rows = field.shape[1] // chunks
    spots = 1 + len(sides)
    lat, lon = lax.axis_index("lat"), lax.axis_index("lon")

    loads = [pltpu.make_async_copy(interp_hbm, interp, weight_sem.at[0])]
    for k in range(field.shape[0]):
        columns = pl.ds(k * width, width)
        loads.append(
            pltpu.make_async_copy(field_hbm.at[:, columns], field.at[k], field_sem.at[k])
        )
    conv_load = pltpu.make_async_copy(conv_hbm, conv, weight_sem.at[1])
    for load in loads:
        load.start()
    conv_load.start()

    def inside(band):
        return jnp.logical_and(band >= 0, band < n_lat)

    def beside(step):
        return lax.rem(lon + step + n_lon, n_lon)

    def lon_first(source, a):
        if a == 1:
            return source == 0
        if a == -1:
            return source == n_lat - 1
        return False

    barrier = pltpu.get_barrier_semaphore()
    for a in STEPS[1:]:

        @pl.when(inside(lat + a))
        def _():
            pl.semaphore_signal(barrier, 1, device_id={"lat": lat + a}, device_id_type=MESH)

    for b in sides:
        pl.semaphore_signal(barrier, 1, device_id={"lon": beside(b)}, device_id_type=MESH)

    def slot(ai, p):
        return pl.ds(tiles + (ai * spots + p) * slots, slots)

    zeros = jnp.zeros((spots * slots, rows, width), jnp.bfloat16)
    for ai, a in enumerate(STEPS):
        if a:

            @pl.when(jnp.logical_not(inside(lat - a)))
            def _():
                for c in range(chunks):
                    readable[c][pl.ds(tiles + ai * spots * slots, spots * slots)] = zeros

    def interpolated(c, k):
        picked = [
            field[blocks_ref[q, k], pl.ds(c * rows, rows)]
            for q in range(feeds)
        ]
        return jnp.dot(
            jnp.concatenate(picked, axis=1), interp[k], preferred_element_type=jnp.float32
        ).astype(jnp.bfloat16)

    def transfer(c, flow, from_ai, from_p, to_ai, to_p, target):
        return pltpu.make_async_remote_copy(
            src_ref=readable[c].at[slot(from_ai, from_p)],
            dst_ref=readable[c].at[slot(to_ai, to_p)],
            send_sem=send_sem.at[flow, c],
            recv_sem=recv_sem.at[to_ai * spots + to_p, c],
            device_id=target,
            device_id_type=MESH,
        )

    def along_lat(c, ai):
        return transfer(c, ai, 0, 0, ai, 0, {"lat": lat + STEPS[ai]})

    def along_lon(c, p):
        return transfer(c, 5 * p, 0, 0, 0, p, {"lon": beside(sides[p - 1])})

    def lat_then_lon(c, ai, p):
        return transfer(c, 5 * p + ai, ai, 0, ai, p, {"lon": beside(sides[p - 1])})

    def lon_then_lat(c, ai, p):
        return transfer(c, 5 * spots + 5 * (p - 1) + ai, 0, p, ai, p, {"lat": lat + STEPS[ai]})

    def received(c, ai, p):
        return transfer(c, 0, ai, p, ai, p, {"lon": beside(1)})

    order = (1, 3, 2, 4)
    for load in loads:
        load.wait()
    for c in range(chunks):
        for h in range(slots):
            value = interpolated(c, list_ref[0, h])
            live = h < jnp.full(value.shape, count_ref[0, 0])
            readable[c][tiles + h] = jnp.where(live, value, jnp.zeros_like(value))
        if c == 0:
            peers = len(sides) + sum(inside(lat + a).astype(jnp.int32) for a in STEPS[1:])
            pl.semaphore_wait(barrier, peers)
        for p in range(1, spots):
            along_lon(c, p).start()
        for ai in order:

            @pl.when(inside(lat + STEPS[ai]))
            def _():
                along_lat(c, ai).start()

    def place(k, n):
        e = near_ref[k, n]
        if spots == 2:
            t = jnp.maximum(e - tiles, 0)
            group = t * 43 // 256
            r = t - group * (3 * slots)
            far = tiles + group * (2 * slots) + r - jnp.where(r >= 2 * slots, slots, 0)
            e = jnp.where(e < tiles, e, far)
        return e

    for c in range(chunks):
        for k in range(tiles):
            readable[c][k] = interpolated(c, k)

    def forward(c):
        for p in range(1, spots):
            received(c, 0, p).wait_recv()
            for ai in (1, 3):

                @pl.when(jnp.logical_and(inside(lat + STEPS[ai]), lon_first(lat, STEPS[ai])))
                def _():
                    lon_then_lat(c, ai, p).start()

        for ai in order:
            a = STEPS[ai]

            @pl.when(inside(lat - a))
            def _():
                received(c, ai, 0).wait_recv()

            @pl.when(jnp.logical_and(inside(lat - a), jnp.logical_not(lon_first(lat - a, a))))
            def _():
                for p in range(1, spots):
                    lat_then_lon(c, ai, p).start()

    def convolve(c):
        for ai in order:

            @pl.when(inside(lat - STEPS[ai]))
            def _():
                for p in range(1, spots):
                    received(c, ai, p).wait_recv()

        part = pl.ds(c * rows, rows)
        for k in range(tiles):
            gathered = jnp.concatenate(
                [readable[c][place(k, n)] for n in range(joins)], axis=1
            )
            out[part, k * width : (k + 1) * width] = jnp.dot(
                gathered, conv[k], preferred_element_type=jnp.float32
            ).astype(jnp.bfloat16)
        pltpu.make_async_copy(out.at[part], out_hbm.at[part], out_sem.at[c]).start()

    for c in range(chunks):
        forward(c)
        if c == 0:
            conv_load.wait()
        else:
            convolve(c - 1)
    convolve(chunks - 1)

    for c in range(chunks):
        for p in range(1, spots):
            along_lon(c, p).wait_send()
        for ai in order:
            a = STEPS[ai]

            @pl.when(inside(lat + a))
            def _():
                along_lat(c, ai).wait_send()

            if abs(a) == 1:

                @pl.when(jnp.logical_and(inside(lat + a), lon_first(lat, a)))
                def _():
                    for p in range(1, spots):
                        lon_then_lat(c, ai, p).wait_send()

            @pl.when(jnp.logical_and(inside(lat - a), jnp.logical_not(lon_first(lat - a, a))))
            def _():
                for p in range(1, spots):
                    lat_then_lon(c, ai, p).wait_send()

        part = pl.ds(c * rows, rows)
        pltpu.make_async_copy(out.at[part], out_hbm.at[part], out_sem.at[c]).wait()


def body(
    n_lat,
    n_lon,
    model_field,
    interp_weights,
    interp_blocks,
    send_list,
    send_count,
    conv_weights,
    neighbours,
):
    members, levels = model_field.shape[:2]
    tiles, feeds, width = interp_weights.shape[2:5]
    joins, slots = conv_weights.shape[3], send_list.shape[2]
    rows = members * levels
    cells = model_field.shape[-1]
    sides = (1,) if n_lon == 2 else (1, -1)
    spots = 1 + len(sides)
    smem = pl.BlockSpec(memory_space=pltpu.SMEM)
    whole = pl.BlockSpec(memory_space=pl.ANY)
    flops = 2 * rows * width * width * tiles * (feeds + joins)
    result = pl.pallas_call(
        functools.partial(kernel, n_lat, n_lon, sides),
        out_shape=jax.ShapeDtypeStruct((rows, tiles * width), jnp.bfloat16),
        in_specs=[smem] * 4 + [whole] * 3,
        out_specs=whole,
        scratch_shapes=[
            pltpu.VMEM((cells // width, rows, width), jnp.bfloat16),
            pltpu.VMEM((tiles, feeds * width, width), jnp.bfloat16),
            pltpu.VMEM((tiles, joins * width, width), jnp.bfloat16),
            pltpu.VMEM((rows, tiles * width), jnp.bfloat16),
            pltpu.SemaphoreType.DMA((cells // width,)),
            pltpu.SemaphoreType.DMA((2,)),
            pltpu.SemaphoreType.DMA((CHUNKS,)),
            pltpu.SemaphoreType.DMA((5 * (2 * spots - 1), CHUNKS)),
            pltpu.SemaphoreType.DMA((5 * spots, CHUNKS)),
        ]
        + [
            pltpu.VMEM((tiles + 5 * spots * slots, rows // CHUNKS, width), jnp.bfloat16)
            for _ in range(CHUNKS)
        ],
        compiler_params=pltpu.CompilerParams(
            collective_id=0, has_side_effects=True, vmem_limit_bytes=32 * 1024 * 1024
        ),
        cost_estimate=pl.CostEstimate(
            flops=flops, bytes_accessed=6 * 1024 * 1024, transcendentals=0
        ),
    )(
        interp_blocks[0, 0].T,
        send_list[0],
        send_count,
        neighbours[0, 0],
        model_field.reshape(rows, cells),
        interp_weights.reshape(tiles, feeds * width, width),
        conv_weights.reshape(tiles, joins * width, width),
    )
    return result.reshape(members, levels, 1, 1, -1)


def solution(mesh):
    return jax.shard_map(
        functools.partial(body, mesh.shape["lat"], mesh.shape["lon"]),
        mesh=mesh,
        in_specs=(
            P("groups", "lev", "lat", "lon", None),
            P("lat", "lon", None, None, None, None),
            P("lat", "lon", None, None),
            P("lat", "lon", None),
            P("lat", "lon"),
            P("lat", "lon", None, None, None, None),
            P("lat", "lon", None, None),
        ),
        out_specs=P("groups", "lev", "lat", "lon", None),
        check_vma=False,
    )
```

```python
import functools

import jax
import jax.numpy as jnp
from jax import lax
from jax.experimental import pallas as pl
from jax.experimental.pallas import tpu as pltpu
from jax.sharding import PartitionSpec as P

MESH = pl.DeviceIdType.MESH
STEPS = (0, 1, 2, -1, -2)
CHUNKS = 2


def kernel(
    n_lat,
    n_lon,
    sides,
    blocks_ref,
    list_ref,
    count_ref,
    near_ref,
    field_hbm,
    interp_hbm,
    conv_hbm,
    out,
    field,
    interp,
    conv,
    field_sem,
    weight_sem,
    send_sem,
    recv_sem,
    *readable,
):
    chunks = len(readable)
    width = interp.shape[-1]
    tiles = interp.shape[0]
    joins = conv.shape[1] // width
    feeds = interp.shape[1] // width
    slots = list_ref.shape[1]
    rows = field.shape[1] // chunks
    spots = 1 + len(sides)
    lat, lon = lax.axis_index("lat"), lax.axis_index("lon")

    loads = [pltpu.make_async_copy(interp_hbm, interp, weight_sem.at[0])]
    for k in range(field.shape[0]):
        columns = pl.ds(k * width, width)
        loads.append(
            pltpu.make_async_copy(field_hbm.at[:, columns], field.at[k], field_sem.at[k])
        )
    conv_load = pltpu.make_async_copy(conv_hbm, conv, weight_sem.at[1])
    for load in loads:
        load.start()
    conv_load.start()

    def inside(band):
        return jnp.logical_and(band >= 0, band < n_lat)

    def beside(step):
        return lax.rem(lon + step + n_lon, n_lon)

    def lon_first(source, a):
        if a == 1:
            return source == 0
        if a == -1:
            return source == n_lat - 1
        return False

    barrier = pltpu.get_barrier_semaphore()
    for a in (1, -1):

        @pl.when(inside(lat + a))
        def _():
            pl.semaphore_signal(barrier, 1, device_id={"lat": lat + a}, device_id_type=MESH)

    for b in sides:
        pl.semaphore_signal(barrier, 1, device_id={"lon": beside(b)}, device_id_type=MESH)

    def slot(ai, p):
        return pl.ds(tiles + (ai * spots + p) * slots, slots)

    zeros = jnp.zeros((spots * slots, rows, width), jnp.bfloat16)
    for ai, a in enumerate(STEPS):
        if a:

            @pl.when(jnp.logical_not(inside(lat - a)))
            def _():
                for c in range(chunks):
                    readable[c][pl.ds(tiles + ai * spots * slots, spots * slots)] = zeros

    def interpolated(c, k):
        picked = [
            field[blocks_ref[q, k], pl.ds(c * rows, rows)]
            for q in range(feeds)
        ]
        return jnp.dot(
            jnp.concatenate(picked, axis=1), interp[k], preferred_element_type=jnp.float32
        ).astype(jnp.bfloat16)

    def transfer(c, flow, from_ai, from_p, to_ai, to_p, target):
        return pltpu.make_async_remote_copy(
            src_ref=readable[c].at[slot(from_ai, from_p)],
            dst_ref=readable[c].at[slot(to_ai, to_p)],
            send_sem=send_sem.at[flow, c],
            recv_sem=recv_sem.at[to_ai * spots + to_p, c],
            device_id=target,
            device_id_type=MESH,
        )

    def along_lat(c, ai):
        near = STEPS[ai] // abs(STEPS[ai])
        from_ai = 0 if STEPS[ai] == near else STEPS.index(near)
        return transfer(c, ai, from_ai, 0, ai, 0, {"lat": lat + near})

    def passes_on(a):
        return jnp.logical_and(inside(lat + a), inside(lat - a))

    def along_lon(c, p):
        return transfer(c, 5 * p, 0, 0, 0, p, {"lon": beside(sides[p - 1])})

    def lat_then_lon(c, ai, p):
        return transfer(c, 5 * p + ai, ai, 0, ai, p, {"lon": beside(sides[p - 1])})

    def lon_then_lat(c, ai, p):
        return transfer(c, 5 * spots + 5 * (p - 1) + ai, 0, p, ai, p, {"lat": lat + STEPS[ai]})

    def received(c, ai, p):
        return transfer(c, 0, ai, p, ai, p, {"lon": beside(1)})

    order = (1, 3, 2, 4)
    near_order, far_order = order[:2], order[2:]
    for load in loads:
        load.wait()
    for c in range(chunks):
        for h in range(slots):
            value = interpolated(c, list_ref[0, h])
            live = h < jnp.full(value.shape, count_ref[0, 0])
            readable[c][tiles + h] = jnp.where(live, value, jnp.zeros_like(value))
        if c == 0:
            peers = len(sides) + sum(inside(lat + a).astype(jnp.int32) for a in (1, -1))
            pl.semaphore_wait(barrier, peers)
        for p in range(1, spots):
            along_lon(c, p).start()
        for ai in near_order:

            @pl.when(inside(lat + STEPS[ai]))
            def _():
                along_lat(c, ai).start()

    def place(k, n):
        e = near_ref[k, n]
        if spots == 2:
            t = jnp.maximum(e - tiles, 0)
            group = t * 43 // 256
            r = t - group * (3 * slots)
            far = tiles + group * (2 * slots) + r - jnp.where(r >= 2 * slots, slots, 0)
            e = jnp.where(e < tiles, e, far)
        return e

    def forward(c):
        for p in range(1, spots):
            received(c, 0, p).wait_recv()
            for ai in (1, 3):

                @pl.when(jnp.logical_and(inside(lat + STEPS[ai]), lon_first(lat, STEPS[ai])))
                def _():
                    lon_then_lat(c, ai, p).start()

        for ai in near_order:
            a = STEPS[ai]

            @pl.when(inside(lat - a))
            def _():
                received(c, ai, 0).wait_recv()

            @pl.when(passes_on(a))
            def _():
                along_lat(c, STEPS.index(2 * a)).start()

            across(c, ai)

    def across(c, ai):
        a = STEPS[ai]

        @pl.when(jnp.logical_and(inside(lat - a), jnp.logical_not(lon_first(lat - a, a))))
        def _():
            for p in range(1, spots):
                lat_then_lon(c, ai, p).start()

    def forward_far(c):
        for ai in far_order:

            @pl.when(inside(lat - STEPS[ai]))
            def _():
                received(c, ai, 0).wait_recv()

            across(c, ai)

    def convolve(c):
        for ai in order:

            @pl.when(inside(lat - STEPS[ai]))
            def _():
                for p in range(1, spots):
                    received(c, ai, p).wait_recv()

        part = pl.ds(c * rows, rows)
        for k in range(tiles):
            gathered = jnp.concatenate(
                [readable[c][place(k, n)] for n in range(joins)], axis=1
            )
            out[part, k * width : (k + 1) * width] = jnp.dot(
                gathered, conv[k], preferred_element_type=jnp.float32
            ).astype(jnp.bfloat16)

    for c in range(chunks + 2):
        if c < chunks:
            forward(c)
        if 1 <= c <= chunks:
            forward_far(c - 1)
        if c < chunks:
            for k in range(tiles):
                readable[c][k] = interpolated(c, k)
        if c == 1:
            conv_load.wait()
        if c >= 2:
            convolve(c - 2)

    for c in range(chunks):
        for p in range(1, spots):
            along_lon(c, p).wait_send()
        for ai in order:
            a = STEPS[ai]

            @pl.when(inside(lat + a) if abs(a) == 1 else passes_on(a // 2))
            def _():
                along_lat(c, ai).wait_send()

            if abs(a) == 1:

                @pl.when(jnp.logical_and(inside(lat + a), lon_first(lat, a)))
                def _():
                    for p in range(1, spots):
                        lon_then_lat(c, ai, p).wait_send()

            @pl.when(jnp.logical_and(inside(lat - a), jnp.logical_not(lon_first(lat - a, a))))
            def _():
                for p in range(1, spots):
                    lat_then_lon(c, ai, p).wait_send()


def body(
    n_lat,
    n_lon,
    model_field,
    interp_weights,
    interp_blocks,
    send_list,
    send_count,
    conv_weights,
    neighbours,
):
    members, levels = model_field.shape[:2]
    tiles, feeds, width = interp_weights.shape[2:5]
    joins, slots = conv_weights.shape[3], send_list.shape[2]
    rows = members * levels
    cells = model_field.shape[-1]
    sides = (1,) if n_lon == 2 else (1, -1)
    spots = 1 + len(sides)
    smem = pl.BlockSpec(memory_space=pltpu.SMEM)
    whole = pl.BlockSpec(memory_space=pltpu.HBM)
    flops = 2 * rows * width * width * tiles * (feeds + joins)
    result = pl.pallas_call(
        functools.partial(kernel, n_lat, n_lon, sides),
        out_shape=jax.ShapeDtypeStruct((rows, tiles * width), jnp.bfloat16),
        in_specs=[smem] * 4 + [whole] * 3,
        out_specs=pl.BlockSpec(memory_space=pltpu.VMEM),
        scratch_shapes=[
            pltpu.VMEM((cells // width, rows, width), jnp.bfloat16),
            pltpu.VMEM((tiles, feeds * width, width), jnp.bfloat16),
            pltpu.VMEM((tiles, joins * width, width), jnp.bfloat16),
            pltpu.SemaphoreType.DMA((cells // width,)),
            pltpu.SemaphoreType.DMA((2,)),
            pltpu.SemaphoreType.DMA((5 * (2 * spots - 1), CHUNKS)),
            pltpu.SemaphoreType.DMA((5 * spots, CHUNKS)),
        ]
        + [
            pltpu.VMEM((tiles + 5 * spots * slots, rows // CHUNKS, width), jnp.bfloat16)
            for _ in range(CHUNKS)
        ],
        compiler_params=pltpu.CompilerParams(
            collective_id=0, has_side_effects=True, vmem_limit_bytes=56 * 1024 * 1024
        ),
        cost_estimate=pl.CostEstimate(
            flops=flops, bytes_accessed=6 * 1024 * 1024, transcendentals=0
        ),
    )(
        interp_blocks[0, 0].T,
        send_list[0],
        send_count,
        neighbours[0, 0],
        model_field.reshape(rows, cells),
        interp_weights.reshape(tiles, feeds * width, width),
        conv_weights.reshape(tiles, joins * width, width),
    )
    return result.reshape(members, levels, 1, 1, -1)


def solution(mesh):
    return jax.shard_map(
        functools.partial(body, mesh.shape["lat"], mesh.shape["lon"]),
        mesh=mesh,
        in_specs=(
            P("groups", "lev", "lat", "lon", None),
            P("lat", "lon", None, None, None, None),
            P("lat", "lon", None, None),
            P("lat", "lon", None),
            P("lat", "lon"),
            P("lat", "lon", None, None, None, None),
            P("lat", "lon", None, None),
        ),
        out_specs=P("groups", "lev", "lat", "lon", None),
        check_vma=False,
    )
```

```python
import functools

import jax
import jax.numpy as jnp
from jax import lax
from jax.experimental import pallas as pl
from jax.experimental.pallas import tpu as pltpu
from jax.sharding import PartitionSpec as P

MESH = pl.DeviceIdType.MESH
STEPS = (0, 1, 2, -1, -2)
CHUNKS = 2


def kernel(
    n_lat,
    n_lon,
    sides,
    blocks_hbm,
    list_hbm,
    count_hbm,
    near_hbm,
    field_hbm,
    interp_hbm,
    conv_hbm,
    out,
    blocks_ref,
    list_ref,
    count_ref,
    near_ref,
    field,
    interp,
    conv,
    index_sem,
    field_sem,
    weight_sem,
    send_sem,
    recv_sem,
    *readable,
):
    chunks = len(readable)
    width = interp.shape[-1]
    tiles = interp.shape[0]
    joins = conv.shape[1] // width
    feeds = interp.shape[1] // width
    slots = list_ref.shape[1]
    rows = field.shape[1] // chunks
    spots = 1 + len(sides)
    lat, lon = lax.axis_index("lat"), lax.axis_index("lon")

    indices = (
        (blocks_hbm, blocks_ref),
        (list_hbm, list_ref),
        (count_hbm, count_ref),
        (near_hbm, near_ref),
    )
    loads = [
        pltpu.make_async_copy(source, target, index_sem.at[i])
        for i, (source, target) in enumerate(indices)
    ]
    loads.append(pltpu.make_async_copy(interp_hbm, interp, weight_sem.at[0]))
    for k in range(field.shape[0]):
        columns = pl.ds(k * width, width)
        loads.append(
            pltpu.make_async_copy(field_hbm.at[:, columns], field.at[k], field_sem.at[k])
        )
    conv_load = pltpu.make_async_copy(conv_hbm, conv, weight_sem.at[1])
    for load in loads:
        load.start()

    def inside(band):
        return jnp.logical_and(band >= 0, band < n_lat)

    def beside(step):
        return lax.rem(lon + step + n_lon, n_lon)

    def lon_first(source, a):
        if a == 1:
            return source == 0
        if a == -1:
            return source == n_lat - 1
        return False

    barrier = pltpu.get_barrier_semaphore()
    for a in (1, -1):

        @pl.when(inside(lat + a))
        def _():
            pl.semaphore_signal(barrier, 1, device_id={"lat": lat + a}, device_id_type=MESH)

    for b in sides:
        pl.semaphore_signal(barrier, 1, device_id={"lon": beside(b)}, device_id_type=MESH)

    def slot(ai, p):
        return pl.ds(tiles + (ai * spots + p) * slots, slots)

    zeros = jnp.zeros((spots * slots, rows, width), jnp.bfloat16)
    for ai, a in enumerate(STEPS):
        if a:

            @pl.when(jnp.logical_not(inside(lat - a)))
            def _():
                for c in range(chunks):
                    readable[c][pl.ds(tiles + ai * spots * slots, spots * slots)] = zeros

    def interpolated(c, k):
        picked = [
            field[blocks_ref[q, k], pl.ds(c * rows, rows)]
            for q in range(feeds)
        ]
        return jnp.dot(
            jnp.concatenate(picked, axis=1), interp[k], preferred_element_type=jnp.float32
        ).astype(jnp.bfloat16)

    def transfer(c, flow, from_ai, from_p, to_ai, to_p, target):
        return pltpu.make_async_remote_copy(
            src_ref=readable[c].at[slot(from_ai, from_p)],
            dst_ref=readable[c].at[slot(to_ai, to_p)],
            send_sem=send_sem.at[flow, c],
            recv_sem=recv_sem.at[to_ai * spots + to_p, c],
            device_id=target,
            device_id_type=MESH,
        )

    def along_lat(c, ai):
        near = STEPS[ai] // abs(STEPS[ai])
        from_ai = 0 if STEPS[ai] == near else STEPS.index(near)
        return transfer(c, ai, from_ai, 0, ai, 0, {"lat": lat + near})

    def passes_on(a):
        return jnp.logical_and(inside(lat + a), inside(lat - a))

    def along_lon(c, p):
        return transfer(c, 5 * p, 0, 0, 0, p, {"lon": beside(sides[p - 1])})

    def lat_then_lon(c, ai, p):
        return transfer(c, 5 * p + ai, ai, 0, ai, p, {"lon": beside(sides[p - 1])})

    def lon_then_lat(c, ai, p):
        return transfer(c, 5 * spots + 5 * (p - 1) + ai, 0, p, ai, p, {"lat": lat + STEPS[ai]})

    def received(c, ai, p):
        return transfer(c, 0, ai, p, ai, p, {"lon": beside(1)})

    order = (1, 3, 2, 4)
    near_order, far_order = order[:2], order[2:]
    for load in loads:
        load.wait()
    conv_load.start()
    for c in range(chunks):
        for h in range(slots):
            value = interpolated(c, list_ref[0, h])
            live = h < jnp.full(value.shape, count_ref[0, 0])
            readable[c][tiles + h] = jnp.where(live, value, jnp.zeros_like(value))
        if c == 0:
            peers = len(sides) + sum(inside(lat + a).astype(jnp.int32) for a in (1, -1))
            pl.semaphore_wait(barrier, peers)
        for p in range(1, spots):
            along_lon(c, p).start()
        for ai in near_order:

            @pl.when(inside(lat + STEPS[ai]))
            def _():
                along_lat(c, ai).start()

    def place(k, n):
        e = near_ref[k, n]
        if spots == 2:
            t = jnp.maximum(e - tiles, 0)
            group = t * 43 // 256
            r = t - group * (3 * slots)
            far = tiles + group * (2 * slots) + r - jnp.where(r >= 2 * slots, slots, 0)
            e = jnp.where(e < tiles, e, far)
        return e

    def forward(c):
        for p in range(1, spots):
            received(c, 0, p).wait_recv()
            for ai in (1, 3):

                @pl.when(jnp.logical_and(inside(lat + STEPS[ai]), lon_first(lat, STEPS[ai])))
                def _():
                    lon_then_lat(c, ai, p).start()

        for ai in near_order:
            a = STEPS[ai]

            @pl.when(inside(lat - a))
            def _():
                received(c, ai, 0).wait_recv()

            @pl.when(passes_on(a))
            def _():
                along_lat(c, STEPS.index(2 * a)).start()

            across(c, ai)

    def across(c, ai):
        a = STEPS[ai]

        @pl.when(jnp.logical_and(inside(lat - a), jnp.logical_not(lon_first(lat - a, a))))
        def _():
            for p in range(1, spots):
                lat_then_lon(c, ai, p).start()

    def forward_far(c):
        for ai in far_order:

            @pl.when(inside(lat - STEPS[ai]))
            def _():
                received(c, ai, 0).wait_recv()

            across(c, ai)

    def convolve(c):
        for ai in order:

            @pl.when(inside(lat - STEPS[ai]))
            def _():
                for p in range(1, spots):
                    received(c, ai, p).wait_recv()

        part = pl.ds(c * rows, rows)
        for k in range(tiles):
            gathered = jnp.concatenate(
                [readable[c][place(k, n)] for n in range(joins)], axis=1
            )
            out[part, k * width : (k + 1) * width] = jnp.dot(
                gathered, conv[k], preferred_element_type=jnp.float32
            ).astype(jnp.bfloat16)

    for c in range(chunks + 2):
        if c < chunks:
            forward(c)
        if 1 <= c <= chunks:
            forward_far(c - 1)
        if c < chunks:
            for k in range(tiles):
                readable[c][k] = interpolated(c, k)
        if c == 1:
            conv_load.wait()
        if c >= 2:
            convolve(c - 2)

    for c in range(chunks):
        for p in range(1, spots):
            along_lon(c, p).wait_send()
        for ai in order:
            a = STEPS[ai]

            @pl.when(inside(lat + a) if abs(a) == 1 else passes_on(a // 2))
            def _():
                along_lat(c, ai).wait_send()

            if abs(a) == 1:

                @pl.when(jnp.logical_and(inside(lat + a), lon_first(lat, a)))
                def _():
                    for p in range(1, spots):
                        lon_then_lat(c, ai, p).wait_send()

            @pl.when(jnp.logical_and(inside(lat - a), jnp.logical_not(lon_first(lat - a, a))))
            def _():
                for p in range(1, spots):
                    lat_then_lon(c, ai, p).wait_send()


def body(
    n_lat,
    n_lon,
    model_field,
    interp_weights,
    interp_blocks,
    send_list,
    send_count,
    conv_weights,
    neighbours,
):
    members, levels = model_field.shape[:2]
    tiles, feeds, width = interp_weights.shape[2:5]
    joins, slots = conv_weights.shape[3], send_list.shape[2]
    rows = members * levels
    cells = model_field.shape[-1]
    sides = (1,) if n_lon == 2 else (1, -1)
    spots = 1 + len(sides)
    whole = pl.BlockSpec(memory_space=pltpu.HBM)
    flops = 2 * rows * width * width * tiles * (feeds + joins)
    result = pl.pallas_call(
        functools.partial(kernel, n_lat, n_lon, sides),
        out_shape=jax.ShapeDtypeStruct((rows, tiles * width), jnp.bfloat16),
        in_specs=[whole] * 7,
        out_specs=pl.BlockSpec(memory_space=pltpu.VMEM),
        scratch_shapes=[
            pltpu.SMEM((feeds, tiles), jnp.int32),
            pltpu.SMEM((1, slots), jnp.int32),
            pltpu.SMEM((1, 1), jnp.int32),
            pltpu.SMEM((tiles, joins), jnp.int32),
            pltpu.VMEM((cells // width, rows, width), jnp.bfloat16),
            pltpu.VMEM((tiles, feeds * width, width), jnp.bfloat16),
            pltpu.VMEM((tiles, joins * width, width), jnp.bfloat16),
            pltpu.SemaphoreType.DMA((4,)),
            pltpu.SemaphoreType.DMA((cells // width,)),
            pltpu.SemaphoreType.DMA((2,)),
            pltpu.SemaphoreType.DMA((5 * (2 * spots - 1), CHUNKS)),
            pltpu.SemaphoreType.DMA((5 * spots, CHUNKS)),
        ]
        + [
            pltpu.VMEM((tiles + 5 * spots * slots, rows // CHUNKS, width), jnp.bfloat16)
            for _ in range(CHUNKS)
        ],
        compiler_params=pltpu.CompilerParams(
            collective_id=0, has_side_effects=True, vmem_limit_bytes=56 * 1024 * 1024
        ),
        cost_estimate=pl.CostEstimate(
            flops=flops, bytes_accessed=6 * 1024 * 1024, transcendentals=0
        ),
    )(
        interp_blocks[0, 0].T,
        send_list[0],
        send_count,
        neighbours[0, 0],
        model_field.reshape(rows, cells),
        interp_weights.reshape(tiles, feeds * width, width),
        conv_weights.reshape(tiles, joins * width, width),
    )
    return result.reshape(members, levels, 1, 1, -1)


def solution(mesh):
    return jax.shard_map(
        functools.partial(body, mesh.shape["lat"], mesh.shape["lon"]),
        mesh=mesh,
        in_specs=(
            P("groups", "lev", "lat", "lon", None),
            P("lat", "lon", None, None, None, None),
            P("lat", "lon", None, None),
            P("lat", "lon", None),
            P("lat", "lon"),
            P("lat", "lon", None, None, None, None),
            P("lat", "lon", None, None),
        ),
        out_specs=P("groups", "lev", "lat", "lon", None),
        check_vma=False,
    )
```

```python
import functools

import jax
import jax.numpy as jnp
from jax import lax
from jax.experimental import pallas as pl
from jax.experimental.pallas import tpu as pltpu
from jax.sharding import PartitionSpec as P

MESH = pl.DeviceIdType.MESH
STEPS = (0, 1, 2, -1, -2)
CHUNKS = 2


def kernel(
    n_lat,
    n_lon,
    sides,
    blocks_hbm,
    list_hbm,
    count_hbm,
    near_hbm,
    field_hbm,
    interp_hbm,
    conv_hbm,
    out,
    blocks_ref,
    list_ref,
    count_ref,
    near_ref,
    field,
    interp,
    conv,
    index_sem,
    field_sem,
    weight_sem,
    send_sem,
    recv_sem,
    *readable,
):
    chunks = len(readable)
    width = interp.shape[-1]
    tiles = interp.shape[0]
    joins = conv.shape[1] // width
    feeds = interp.shape[1] // width
    slots = list_ref.shape[1]
    rows = field.shape[1] // chunks
    spots = 1 + len(sides)
    lat, lon = lax.axis_index("lat"), lax.axis_index("lon")

    indices = (
        (blocks_hbm, blocks_ref),
        (list_hbm, list_ref),
        (count_hbm, count_ref),
        (near_hbm, near_ref),
    )
    loads = [
        pltpu.make_async_copy(source, target, index_sem.at[i])
        for i, (source, target) in enumerate(indices)
    ]
    loads.append(pltpu.make_async_copy(interp_hbm, interp, weight_sem.at[0]))
    for k in range(field.shape[0]):
        columns = pl.ds(k * width, width)
        loads.append(
            pltpu.make_async_copy(field_hbm.at[:, columns], field.at[k], field_sem.at[k])
        )
    conv_load = pltpu.make_async_copy(conv_hbm, conv, weight_sem.at[1])
    for load in loads:
        load.start()

    def inside(band):
        return jnp.logical_and(band >= 0, band < n_lat)

    def beside(step):
        return lax.rem(lon + step + n_lon, n_lon)

    def lon_first(source, a):
        if a == 1:
            return source == 0
        if a == -1:
            return source == n_lat - 1
        return False

    barrier = pltpu.get_barrier_semaphore()
    for a in (1, -1):

        @pl.when(inside(lat + a))
        def _():
            pl.semaphore_signal(barrier, 1, device_id={"lat": lat + a}, device_id_type=MESH)

    for b in sides:
        pl.semaphore_signal(barrier, 1, device_id={"lon": beside(b)}, device_id_type=MESH)

    def slot(ai, p):
        return pl.ds(tiles + (ai * spots + p) * slots, slots)

    zeros = jnp.zeros((spots * slots, rows, width), jnp.bfloat16)
    for ai, a in enumerate(STEPS):
        if a:

            @pl.when(jnp.logical_not(inside(lat - a)))
            def _():
                for c in range(chunks):
                    readable[c][pl.ds(tiles + ai * spots * slots, spots * slots)] = zeros

    def interpolated(c, k):
        picked = [
            field[blocks_ref[q, k], pl.ds(c * rows, rows)]
            for q in range(feeds)
        ]
        return jnp.dot(
            jnp.concatenate(picked, axis=1), interp[k], preferred_element_type=jnp.float32
        ).astype(jnp.bfloat16)

    def transfer(c, flow, from_ai, from_p, to_ai, to_p, target):
        return pltpu.make_async_remote_copy(
            src_ref=readable[c].at[slot(from_ai, from_p)],
            dst_ref=readable[c].at[slot(to_ai, to_p)],
            send_sem=send_sem.at[flow, c],
            recv_sem=recv_sem.at[to_ai * spots + to_p, c],
            device_id=target,
            device_id_type=MESH,
        )

    def along_lat(c, ai):
        near = STEPS[ai] // abs(STEPS[ai])
        from_ai = 0 if STEPS[ai] == near else STEPS.index(near)
        return transfer(c, ai, from_ai, 0, ai, 0, {"lat": lat + near})

    def passes_on(a):
        return jnp.logical_and(inside(lat + a), inside(lat - a))

    def along_lon(c, p):
        return transfer(c, 5 * p, 0, 0, 0, p, {"lon": beside(sides[p - 1])})

    def lat_then_lon(c, ai, p):
        return transfer(c, 5 * p + ai, ai, 0, ai, p, {"lon": beside(sides[p - 1])})

    def lon_then_lat(c, ai, p):
        return transfer(c, 5 * spots + 5 * (p - 1) + ai, 0, p, ai, p, {"lat": lat + STEPS[ai]})

    def received(c, ai, p):
        return transfer(c, 0, ai, p, ai, p, {"lon": beside(1)})

    order = (1, 3, 2, 4)
    near_order, far_order = order[:2], order[2:]
    for load in loads:
        load.wait()
    conv_load.start()
    for c in range(chunks):
        for h in range(slots):
            value = interpolated(c, list_ref[0, h])
            live = h < jnp.full(value.shape, count_ref[0, 0])
            readable[c][tiles + h] = jnp.where(live, value, jnp.zeros_like(value))
        if c == 0:
            peers = len(sides) + sum(inside(lat + a).astype(jnp.int32) for a in (1, -1))
            pl.semaphore_wait(barrier, peers)
        for ai in near_order:

            @pl.when(inside(lat + STEPS[ai]))
            def _():
                along_lat(c, ai).start()

        for p in range(1, spots):
            along_lon(c, p).start()

    def place(k, n):
        e = near_ref[k, n]
        if spots == 2:
            t = jnp.maximum(e - tiles, 0)
            group = t * 43 // 256
            r = t - group * (3 * slots)
            far = tiles + group * (2 * slots) + r - jnp.where(r >= 2 * slots, slots, 0)
            e = jnp.where(e < tiles, e, far)
        return e

    def forward(c):
        for p in range(1, spots):
            received(c, 0, p).wait_recv()
            for ai in (1, 3):

                @pl.when(jnp.logical_and(inside(lat + STEPS[ai]), lon_first(lat, STEPS[ai])))
                def _():
                    lon_then_lat(c, ai, p).start()

        for ai in near_order:
            a = STEPS[ai]

            @pl.when(inside(lat - a))
            def _():
                received(c, ai, 0).wait_recv()

            @pl.when(passes_on(a))
            def _():
                along_lat(c, STEPS.index(2 * a)).start()

            across(c, ai)

    def across(c, ai):
        a = STEPS[ai]

        @pl.when(jnp.logical_and(inside(lat - a), jnp.logical_not(lon_first(lat - a, a))))
        def _():
            for p in range(1, spots):
                lat_then_lon(c, ai, p).start()

    def forward_far(c):
        for ai in far_order:

            @pl.when(inside(lat - STEPS[ai]))
            def _():
                received(c, ai, 0).wait_recv()

            across(c, ai)

    def convolve(c):
        for ai in order:

            @pl.when(inside(lat - STEPS[ai]))
            def _():
                for p in range(1, spots):
                    received(c, ai, p).wait_recv()

        part = pl.ds(c * rows, rows)
        for k in range(tiles):
            gathered = jnp.concatenate(
                [readable[c][place(k, n)] for n in range(joins)], axis=1
            )
            out[part, k * width : (k + 1) * width] = jnp.dot(
                gathered, conv[k], preferred_element_type=jnp.float32
            ).astype(jnp.bfloat16)

    for c in range(chunks + 2):
        if c < chunks:
            forward(c)
        if 1 <= c <= chunks:
            forward_far(c - 1)
        if c < chunks:
            for k in range(tiles):
                readable[c][k] = interpolated(c, k)
        if c == 1:
            conv_load.wait()
        if c >= 2:
            convolve(c - 2)

    for c in range(chunks):
        for p in range(1, spots):
            along_lon(c, p).wait_send()
        for ai in order:
            a = STEPS[ai]

            @pl.when(inside(lat + a) if abs(a) == 1 else passes_on(a // 2))
            def _():
                along_lat(c, ai).wait_send()

            if abs(a) == 1:

                @pl.when(jnp.logical_and(inside(lat + a), lon_first(lat, a)))
                def _():
                    for p in range(1, spots):
                        lon_then_lat(c, ai, p).wait_send()

            @pl.when(jnp.logical_and(inside(lat - a), jnp.logical_not(lon_first(lat - a, a))))
            def _():
                for p in range(1, spots):
                    lat_then_lon(c, ai, p).wait_send()


def body(
    n_lat,
    n_lon,
    model_field,
    interp_weights,
    interp_blocks,
    send_list,
    send_count,
    conv_weights,
    neighbours,
):
    members, levels = model_field.shape[:2]
    tiles, feeds, width = interp_weights.shape[2:5]
    joins, slots = conv_weights.shape[3], send_list.shape[2]
    rows = members * levels
    cells = model_field.shape[-1]
    sides = (1,) if n_lon == 2 else (1, -1)
    spots = 1 + len(sides)
    whole = pl.BlockSpec(memory_space=pltpu.HBM)
    flops = 2 * rows * width * width * tiles * (feeds + joins)
    result = pl.pallas_call(
        functools.partial(kernel, n_lat, n_lon, sides),
        out_shape=jax.ShapeDtypeStruct((rows, tiles * width), jnp.bfloat16),
        in_specs=[whole] * 7,
        out_specs=pl.BlockSpec(memory_space=pltpu.VMEM),
        scratch_shapes=[
            pltpu.SMEM((feeds, tiles), jnp.int32),
            pltpu.SMEM((1, slots), jnp.int32),
            pltpu.SMEM((1, 1), jnp.int32),
            pltpu.SMEM((tiles, joins), jnp.int32),
            pltpu.VMEM((cells // width, rows, width), jnp.bfloat16),
            pltpu.VMEM((tiles, feeds * width, width), jnp.bfloat16),
            pltpu.VMEM((tiles, joins * width, width), jnp.bfloat16),
            pltpu.SemaphoreType.DMA((4,)),
            pltpu.SemaphoreType.DMA((cells // width,)),
            pltpu.SemaphoreType.DMA((2,)),
            pltpu.SemaphoreType.DMA((5 * (2 * spots - 1), CHUNKS)),
            pltpu.SemaphoreType.DMA((5 * spots, CHUNKS)),
        ]
        + [
            pltpu.VMEM((tiles + 5 * spots * slots, rows // CHUNKS, width), jnp.bfloat16)
            for _ in range(CHUNKS)
        ],
        compiler_params=pltpu.CompilerParams(
            collective_id=0, has_side_effects=True, vmem_limit_bytes=56 * 1024 * 1024
        ),
        cost_estimate=pl.CostEstimate(
            flops=flops, bytes_accessed=6 * 1024 * 1024, transcendentals=0
        ),
    )(
        interp_blocks[0, 0].T,
        send_list[0],
        send_count,
        neighbours[0, 0],
        model_field.reshape(rows, cells),
        interp_weights.reshape(tiles, feeds * width, width),
        conv_weights.reshape(tiles, joins * width, width),
    )
    return result.reshape(members, levels, 1, 1, -1)


def solution(mesh):
    return jax.shard_map(
        functools.partial(body, mesh.shape["lat"], mesh.shape["lon"]),
        mesh=mesh,
        in_specs=(
            P("groups", "lev", "lat", "lon", None),
            P("lat", "lon", None, None, None, None),
            P("lat", "lon", None, None),
            P("lat", "lon", None),
            P("lat", "lon"),
            P("lat", "lon", None, None, None, None),
            P("lat", "lon", None, None),
        ),
        out_specs=P("groups", "lev", "lat", "lon", None),
        check_vma=False,
    )
```
